768 devices in a mesh: dp: 64 (over z_hi, y, x), tensor: 12 (over z_lo, core).
Axes of the slice: x: 4, y: 8, z: 12 (z_hi: 2, z_lo: 6; z = z_hi * 6 + z_lo), core: 2. Of those that a mesh axis runs over, the one named last changes fastest.
Arguments:
- mantissas: bfloat16 [12288, 3072], P(('dp', 'tensor')), may hold values from -24 to 24
- exponents: int32 [12288, 24], P(('dp', 'tensor')), may hold values from -3 to 1
- weight: bfloat16 [3072, 7680], P(None, 'tensor'), may hold values from -0.109375 to 0.109375
- cotangent: bfloat16 [12288, 7680], P('dp', 'tensor'), may hold values from -16 to 16
Outputs:
- output: bfloat16 [12288, 7680], P('dp', 'tensor')
- grad_input: bfloat16 [12288, 3072], P(('dp', 'tensor'))
- grad_weight: float32 [3072, 7680], P('dp', 'tensor')
The draws below stay inside these ranges and needn't reach their ends.
Inputs may be any that keep to these rules, and one draw needn't show every extreme that they name: `exponents`: base-two exponent of a block of 128 features.
All inputs are finite; a program needn't handle non-finite values.
Results may differ from the reference program's by a relative error of at most 0.02.
Values may be sent and summed in bfloat16 or wider, within the bound.
A program may use at most 64 MiB of HBM per device.

```python
import math
import jax
import jax.numpy as jnp
from jax import lax

D = 3072
FF_DEV = 640
FF = 7680
TOKENS = 12288
N_TENSOR = 12


def set_ends(result, own_key, least, top_value):
    longest = result.shape.index(max(result.shape))
    spots = []
    for shift in (0, 1):
        where = [jax.random.randint(jax.random.fold_in(own_key, axis), (), 0, length) for axis, length in enumerate(result.shape)]
        where[longest] = (where[longest] + shift) % result.shape[longest]
        spots.append(tuple(where))
    return result.at[spots[0]].set(least).at[spots[1]].set(top_value)


def with_spikes(array, stream_key, source, target, shards_of, factor):
    owner, partner = [(jnp.arange(array.shape[dim]) // (array.shape[dim] // shards_of)).reshape([-1 if axis == dim else 1 for axis in range(array.ndim)]) for dim in (source, target)]
    chosen = jax.random.permutation(stream_key, shards_of)[partner]
    strong = (owner == chosen) | (owner == (partner + shards_of // 2) % shards_of)
    return jnp.where(strong, factor * array, array)


def shard_levels(own_key, dims, cuts, low, largest):
    level = 1.0
    for dim, blocks in cuts:
        steps = jax.random.uniform(jax.random.fold_in(jax.random.fold_in(own_key, 6), dim), (blocks,), jnp.float32, low / len(cuts), largest / len(cuts))
        level = level * jnp.repeat(jnp.exp(steps), dims[dim] // blocks).reshape((-1,) + (1,) * (len(dims) - 1 - dim))
    return level


def centred(stream_key, dims, spread, most, cuts=(), held_as=jnp.bfloat16):
    drawn = jax.random.normal(stream_key, dims, jnp.float32) * spread
    if len(cuts) > 0:
        drawn = shard_levels(stream_key, dims, cuts, -0.22, 0.18) * drawn
    return jnp.clip(drawn, min=-most, max=most).astype(held_as)


def gaussian_with(key, dims, deviation, most, cuts, heavy, dtype=jnp.bfloat16):
    result = deviation * jax.random.normal(key, dims, jnp.float32)
    if cuts:
        result = result * shard_levels(key, dims, cuts, -0.22, 0.18)
    return jnp.clip(with_spikes(result, jax.random.fold_in(key, 3), *heavy), -most, most).astype(dtype)


def setup_inputs(seed: int = 0) -> dict:
    splits = jax.random.split(jax.random.key(seed), 5)
    mantissas = gaussian_with(splits[0], (TOKENS, D), 1.0, 24.0, ((0, 768),), (0, 1, 768, 6.0))
    exponents = set_ends(jax.random.randint(splits[1], (TOKENS, D // 128), -3, 2), jax.random.fold_in(splits[1], 1), -3, 1).astype(jnp.int32)
    weight = centred(splits[2], (D, FF), D ** -0.5, 0.109375, ((1, 12),))
    cotangent = gaussian_with(splits[3], (TOKENS, FF), 1.0, 16.0, ((0, 64), (1, 12)), (1, 0, 64, 4.0))
    return dict(mantissas=mantissas, exponents=exponents, weight=weight, cotangent=cotangent)


def reference(mantissas, exponents, weight, cotangent):
    factors = jnp.exp2(exponents.astype(jnp.float32))
    blocks = mantissas.astype(jnp.float32).reshape(TOKENS, D // 128, 128) * factors[:, :, None]
    inputs = blocks.reshape(TOKENS, D).astype(jnp.bfloat16)
    linear = jnp.dot(inputs, weight, preferred_element_type=jnp.float32)
    output = jax.nn.silu(linear).astype(jnp.bfloat16)
    sigmoid = jax.nn.sigmoid(linear)
    grad_linear = (cotangent.astype(jnp.float32) * sigmoid * (1.0 + linear * (1.0 - sigmoid))).astype(jnp.bfloat16)
    summed = jnp.zeros((TOKENS, D), jnp.float32)
    for member in range(N_TENSOR):
        part_grad = grad_linear[:, member * FF_DEV:(member + 1) * FF_DEV]
        part_weight = weight[:, member * FF_DEV:(member + 1) * FF_DEV]
        partial_sum = lax.dot_general(part_grad, part_weight, (((1,), (1,)), ((), ())), preferred_element_type=jnp.float32)
        rounded = lax.optimization_barrier(partial_sum.astype(jnp.bfloat16))
        summed = summed + rounded.astype(jnp.float32)
    grad_input = summed.astype(jnp.bfloat16)
    grad_weight = lax.dot_general(inputs, grad_linear, (((0,), (0,)), ((), ())), preferred_element_type=jnp.float32)
    grad_weight = grad_weight * (1.0 / math.sqrt(TOKENS))
    return (output, grad_input, grad_weight)
```

```python
import functools
import math
from types import SimpleNamespace

import jax
import jax.numpy as jnp
from jax import lax
from jax.experimental import pallas as pl
from jax.experimental.pallas import tpu as pltpu
from jax.sharding import PartitionSpec as P

MESH = pl.DeviceIdType.MESH
F32, BF16 = jnp.float32, jnp.bfloat16

SIZES = SimpleNamespace(H=2, Y=8, X=4, Z=6, C=2, B=16, R=48, F=640)


def permute_tiles(tiles, size, out_chunk_source):
    lane = lax.broadcasted_iota(jnp.int32, tiles[0].shape, 1)
    result = []
    for k in range(len(tiles)):
        runs = []
        for l in range(128):
            o = k * 128 + l
            src = out_chunk_source(o // size) * size + o % size
            key = (src // 128, (l - src) % 128)
            if runs and runs[-1][0] == key:
                runs[-1][2] = l + 1
            else:
                runs.append([key, l, l + 1])
        out = None
        for (tile, shift), lo, hi in runs:
            piece = tiles[tile]
            if shift:
                piece = pltpu.roll(piece, shift, 1)
            out = piece if out is None else jnp.where(lane >= lo, piece, out)
        result.append(out)
    return result


def kernel(
    n,
    mant, expo, w_hbm, ct_hbm,
    out_hbm, dx_out, dw_out,
    wp, wn, ct, xg, lin, xq, gq, outv, prt, psib, rr, rl, sr, sl, acc, ysend, yrecv, tu, hsend, hrecv,
    loc, ag_s, ag_r, sib_s, sib_r, xs_s, xs_r, xb_s, xb_r, g_s, g_r, p_s, p_r, dx_s, dx_r, y_s, y_r, h_s, h_r,
):
    H, Y, X, Z, C, B, R, F = n.H, n.Y, n.X, n.Z, n.C, n.B, n.R, n.F
    HY = H * Y
    D = HY * X * R
    Q = D // X
    TH = Z * B
    T = C * TH
    S = n.S
    SB = D // S
    YH = Y // 2

    dp = lax.axis_index("dp")
    tp = lax.axis_index("tensor")
    x = lax.rem(dp, X)
    y = lax.rem(dp // X, Y)
    h = dp // (X * Y)
    c = lax.rem(tp, C)
    z = tp // C
    plane = dp - x

    sib = (dp, tp + 1 - 2 * c)
    z_right = (dp, tp + C)
    z_left = (dp, tp - C)
    x_by = {k: (plane + lax.rem(x + k, X), tp) for k in (1, 2, 3)}
    y_by = [
        ((h * Y + lax.rem(y + 1, Y)) * X + x, tp),
        ((h * Y + lax.rem(y + Y - 1, Y)) * X + x, tp),
    ]
    h_by = (((1 - h) * Y + y) * X + x, tp)

    def remote(src, dst, send, recv, device):
        return pltpu.make_async_remote_copy(
            src_ref=src, dst_ref=dst, send_sem=send, recv_sem=recv,
            device_id=device, device_id_type=MESH,
        )

    def arrived(dst, recv):
        remote(dst, dst, recv, recv, sib).wait_recv()

    def sent(src, send):
        remote(src, src, send, send, sib).wait_send()

    barrier = pltpu.get_barrier_semaphore()
    ring = [
        (dp, lax.rem(tp + C, Z * C)),
        (dp, lax.rem(tp + Z * C - C, Z * C)),
    ]
    greeted = [sib, *ring, x_by[1], x_by[2], x_by[3], *y_by, h_by]
    for device in greeted:
        pl.semaphore_signal(barrier, inc=1, device_id=device, device_id_type=MESH)

    w_in = [pltpu.make_async_copy(w_hbm.at[:, k], wp.at[k], loc.at[k]) for k in range(X)]
    ct_in = [pltpu.make_async_copy(ct_hbm.at[:, k], ct.at[k], loc.at[X + k]) for k in range(C)]
    wn_in = pltpu.make_async_copy(w_hbm, wn, loc.at[X + C])
    for copy in [*w_in, *ct_in, wn_in]:
        copy.start()

    def rows(core, q):
        return pl.ds(pl.multiple_of(core * TH + q * B, B), B)

    factors = jnp.exp2(expo[...].astype(F32))
    tiles = [
        mant[:, pl.ds(128 * b, 128)].astype(F32) * factors[:, b : b + 1]
        for b in range(D // 128)
    ]
    for k, tile in enumerate(permute_tiles(tiles, R, lambda j: (j % HY) * X + j // HY)):
        xg[rows(c, z), pl.ds(128 * k, 128)] = tile.astype(BF16)

    pl.semaphore_wait(barrier, len(greeted))

    def hop(way, step, sub, q):
        part = xg.at[rows(c, q), pl.ds(sub * SB, SB)]
        return remote(
            part, part, ag_s.at[way, step, sub], ag_r.at[way, step, sub],
            z_right if way == 0 else z_left,
        )

    def spread_sibling(q):
        part = xg.at[rows(c, q), :]
        return remote(part, part, sib_s.at[q], sib_r.at[q], sib)

    def spread_x(q, k):
        to = lax.rem(x + k, X)
        return remote(
            xg.at[rows(c, q), pl.ds(pl.multiple_of(to * Q, Q), Q)],
            xq.at[k - 1, rows(c, q), :],
            xs_s.at[k - 1], xs_r.at[k - 1], x_by[k],
        )

    def spread(q):
        spread_sibling(q).start()
        for k in (1, 3, 2):
            spread_x(q, k).start()

    for sub in range(S):
        @pl.when(z < Z - 1)
        def _():
            hop(0, 0, sub, z).start()

        @pl.when(z > 0)
        def _():
            hop(1, 0, sub, z).start()

    spread(z)
    for s in range(Z - 1):
        from_left = z - 1 - s
        from_right = z + 1 + s
        for sub in range(S):
            @pl.when(from_left >= 0)
            def _():
                hop(0, s, sub, from_left).wait_recv()
                if s + 1 < Z - 1:
                    @pl.when(z < Z - 1)
                    def _():
                        hop(0, s + 1, sub, from_left).start()

            @pl.when(from_right <= Z - 1)
            def _():
                hop(1, s, sub, from_right).wait_recv()
                if s + 1 < Z - 1:
                    @pl.when(z > 0)
                    def _():
                        hop(1, s + 1, sub, from_right).start()

        @pl.when(from_left >= 0)
        def _():
            spread(from_left)

        @pl.when(from_right <= Z - 1)
        def _():
            spread(from_right)

    for q in range(Z):
        arrived(xg.at[rows(1 - c, q), :], sib_r.at[q])

    for k in range(X):
        w_in[k].wait()
        part = jnp.dot(
            xg[:, pl.ds(k * Q, Q)], wp[k].reshape(Q, F), preferred_element_type=F32
        )
        if k == 0:
            lin[...] = part
        else:
            lin[...] += part
    for copy in ct_in:
        copy.wait()
    linear = lin[...]
    sigmoid = jax.nn.sigmoid(linear)
    cot = ct[...].reshape(T, F).astype(F32)
    gq[0] = (cot * sigmoid * (1.0 + linear * (1.0 - sigmoid))).astype(BF16)

    def g_part(i):
        slot, half, k = [(1, 0, 1), (3, 1, 3), (1, 1, 1), (3, 0, 3)][i]
        where = pl.ds(half * TH, TH)
        return remote(gq.at[0, where], gq.at[slot, where], g_s.at[i], g_r.at[i], x_by[k])

    def g_forward(i):
        where = pl.ds(i * TH, TH)
        return remote(
            gq.at[1 if i == 0 else 3, where], gq.at[2, where], g_s.at[4 + i], g_r.at[4 + i],
            x_by[1 if i == 0 else 3],
        )

    for i in range(4):
        g_part(i).start()

    outv[...] = (linear * sigmoid).astype(BF16).reshape(C, Z, B, F)
    out_back = [
        pltpu.make_async_copy(outv.at[k], out_hbm.at[:, k], loc.at[X + C + 1 + k]) for k in range(C)
    ]
    for copy in out_back:
        copy.start()

    def x_sibling(k):
        part = xq.at[k - 1, pl.ds(pl.multiple_of(c * TH, TH), TH), :]
        return remote(part, part, xb_s.at[k - 1], xb_r.at[k - 1], sib)

    for k in (1, 3, 2):
        arrived(xq.at[k - 1, pl.ds(0, TH), :], xs_r.at[k - 1])
        x_sibling(k).start()

    wn_in.wait()
    NC = X
    ND = D // NC

    def p_sibling(k):
        columns = pl.ds(k * ND, ND)
        return remote(
            prt.at[pl.ds(pl.multiple_of((1 - c) * TH, TH), TH), columns], psib.at[:, columns],
            p_s.at[k], p_r.at[k], sib,
        )

    for k in range(NC):
        part = lax.dot_general(
            gq[0], wn[pl.ds(k * (HY // NC), HY // NC)].reshape(ND, F),
            (((1,), (1,)), ((), ())), preferred_element_type=F32,
        )
        prt[:, pl.ds(k * ND, ND)] = part.astype(BF16)
        p_sibling(k).start()

    for i in range(2):
        g_part(i).wait_recv()
        g_forward(i).start()

    for k in range(NC):
        p_sibling(k).wait_recv()

    def pair(q):
        own = prt[rows(c, q), :].astype(F32)
        return own + psib[pl.ds(pl.multiple_of(q * B, B), B), :].astype(F32)

    def dx_hop(way, j):
        return remote(
            (sr, sl)[way].at[j], (rr, rl)[way].at[j], dx_s.at[way, j], dx_r.at[way, j],
            (z_right, z_left)[way],
        )

    def dx_slot(t):
        for way, first in ((0, z), (1, Z - 1 - z)):
            j = t - first
            q = Z - 1 - j if way == 0 else j
            out, came = (sr, sl)[way], (rr, rl)[way]

            @pl.when(first == 0)
            def _():
                out[j] = pair(q).astype(BF16)
                dx_hop(way, j).start()

            if t > 0:
                @pl.when((first > 0) & (j >= 0))
                def _():
                    dx_hop(way, j).wait_recv()
                    out[j] = (pair(q) + came[j].astype(F32)).astype(BF16)
                    dx_hop(way, j).start()

    def dw_slot(k):
        if k == 0:
            left = xg[:, pl.ds(pl.multiple_of(x * Q, Q), Q)]
        else:
            left = xq[k - 1]
        part = lax.dot_general(
            left, gq[k], (((0,), (0,)), ((), ())), preferred_element_type=F32
        )
        if k == 0:
            acc[...] = part
        else:
            acc[...] += part

    dx_slot(0)
    dw_slot(0)
    for k in (1, 3, 2):
        x_sibling(k).wait_recv()
    g_part(2).wait_recv()
    dw_slot(1)
    if Z > 2:
        dx_slot(1)
    g_part(3).wait_recv()
    dw_slot(3)
    for i in range(2):
        g_forward(i).wait_recv()
    dw_slot(2)

    def y_hop(way, u, s):
        return remote(
            ysend.at[way, u, s - 1], yrecv.at[way, u, s - 1],
            y_s.at[way, u, s - 1], y_r.at[way, u, s - 1], y_by[way],
        )

    def y_rows(u, to):
        return pl.ds(pl.multiple_of((u * Y + to) * R, R), R)

    def first_step(way, u):
        return 1 if way == u else 2

    def y_step(s):
        for i in range(2):
            for way in range(2):
                u = way if i == 0 else 1 - way
                start = first_step(way, u)
                if s < start or s > YH:
                    continue
                away = YH + 1 - s
                to = lax.rem(y + (away if way == 0 else Y - away), Y)
                value = acc[y_rows(u, to), :]
                if s > start:
                    y_hop(way, u, s - 1).wait_recv()
                    value = value + yrecv[way, u, s - 2].astype(F32)
                ysend[way, u, s - 1] = value.astype(BF16)
                y_hop(way, u, s).start()

    slot = 2
    for s in range(1, YH + 1):
        y_step(s)
        if slot < Z - 1:
            dx_slot(slot)
            slot += 1
    while slot < Z - 1:
        dx_slot(slot)
        slot += 1

    for u in range(H):
        value = acc[y_rows(u, y), :]
        for way in range(2):
            if first_step(way, u) <= YH:
                y_hop(way, u, YH).wait_recv()
                value = value + yrecv[way, u, YH - 1].astype(F32)
        tu[u] = value
    hsend[...] = tu[1 - h].astype(BF16)
    across = remote(hsend, hrecv, h_s, h_r, h_by)
    across.start()

    lin_dx = pair(z)

    @pl.when(z == 0)
    def _():
        arrived(rl.at[0], dx_r.at[1, 0])
        dx_out[...] = (lin_dx + rl[0].astype(F32)).astype(BF16)

    @pl.when(z == Z - 1)
    def _():
        arrived(rr.at[0], dx_r.at[0, 0])
        dx_out[...] = (lin_dx + rr[0].astype(F32)).astype(BF16)

    @pl.when((z > 0) & (z < Z - 1))
    def _():
        arrived(rr.at[Z - 1 - z], dx_r.at[0, Z - 1 - z])
        arrived(rl.at[z], dx_r.at[1, z])
        dx_out[...] = (lin_dx + rr[Z - 1 - z].astype(F32) + rl[z].astype(F32)).astype(BF16)

    across.wait_recv()
    factor = 1.0 / math.sqrt(H * Y * X * T)
    dw_out[...] = (tu[h] + hrecv[...].astype(F32)) * factor

    for copy in out_back:
        copy.wait()
    for sub in range(S):
        for s in range(Z - 1):
            @pl.when((z - s >= 0) & (z < Z - 1))
            def _():
                hop(0, s, sub, z - s).wait_send()

            @pl.when((z + s <= Z - 1) & (z > 0))
            def _():
                hop(1, s, sub, z + s).wait_send()
    for q in range(Z):
        spread_sibling(q).wait_send()
    for k in (1, 2, 3):
        sent(xq.at[k - 1, pl.ds(0, TH), :], xs_s.at[k - 1])
        x_sibling(k).wait_send()
    for i in range(4):
        g_part(i).wait_send()
    for i in range(2):
        g_forward(i).wait_send()
    for k in range(NC):
        p_sibling(k).wait_send()
    for j in range(Z - 1):
        @pl.when(Z - 1 - j > z)
        def _():
            dx_hop(0, j).wait_send()

        @pl.when(j < z)
        def _():
            dx_hop(1, j).wait_send()
    for way in range(2):
        for u in range(2):
            for s in range(first_step(way, u), YH + 1):
                y_hop(way, u, s).wait_send()
    across.wait_send()


def body(n, mantissas, exponents, weight, cotangent):
    H, Y, X, Z, C, B, R, F = n.H, n.Y, n.X, n.Z, n.C, n.B, n.R, n.F
    HY = H * Y
    D = HY * X * R
    Q, TH, T, S, YH = D // X, Z * B, Z * B * C, n.S, Y // 2
    anywhere = pl.BlockSpec(memory_space=pl.ANY)
    vmem = pl.BlockSpec(memory_space=pltpu.VMEM)
    dma = pltpu.SemaphoreType.DMA
    out, dx, dw = pl.pallas_call(
        functools.partial(kernel, n),
        out_shape=(
            jax.ShapeDtypeStruct((Z, C, B, F), BF16),
            jax.ShapeDtypeStruct((B, D), BF16),
            jax.ShapeDtypeStruct((R, F), F32),
        ),
        in_specs=[vmem, vmem, anywhere, anywhere],
        out_specs=(anywhere, vmem, vmem),
        scratch_shapes=[
            pltpu.VMEM((X, HY, R, F), BF16),
            pltpu.VMEM((HY, X, R, F), BF16),
            pltpu.VMEM((C, Z, B, F), BF16),
            pltpu.VMEM((T, D), BF16),
            pltpu.VMEM((T, F), F32),
            pltpu.VMEM((3, T, Q), BF16),
            pltpu.VMEM((4, T, F), BF16),
            pltpu.VMEM((C, Z, B, F), BF16),
            pltpu.VMEM((T, D), BF16),
            pltpu.VMEM((TH, D), BF16),
            pltpu.VMEM((Z - 1, B, D), BF16),
            pltpu.VMEM((Z - 1, B, D), BF16),
            pltpu.VMEM((Z - 1, B, D), BF16),
            pltpu.VMEM((Z - 1, B, D), BF16),
            pltpu.VMEM((Q, F), F32),
            pltpu.VMEM((2, 2, YH, R, F), BF16),
            pltpu.VMEM((2, 2, YH, R, F), BF16),
            pltpu.VMEM((2, R, F), F32),
            pltpu.VMEM((R, F), BF16),
            pltpu.VMEM((R, F), BF16),
            dma((X + 2 * C + 1,)),
            dma((2, Z, S)),
            dma((2, Z, S)),
            dma((Z,)),
            dma((Z,)),
            dma((3,)),
            dma((3,)),
            dma((3,)),
            dma((3,)),
            dma((6,)),
            dma((6,)),
            dma((X,)),
            dma((X,)),
            dma((2, Z - 1)),
            dma((2, Z - 1)),
            dma((2, 2, YH)),
            dma((2, 2, YH)),
            dma,
            dma,
        ],
        compiler_params=pltpu.CompilerParams(
            collective_id=0, has_side_effects=True, vmem_limit_bytes=50 * 1024 * 1024
        ),
        cost_estimate=pl.CostEstimate(
            flops=6 * T * D * F, bytes_accessed=4 * D * F, transcendentals=T * F
        ),
    )(
        mantissas,
        exponents,
        weight.reshape(HY, X, R, F),
        cotangent.reshape(Z, C, B, F),
    )
    return out.reshape(T, F), dx, dw


def solution(mesh, sizes=SIZES):
    n = SimpleNamespace(**vars(sizes), S=4)
    return jax.shard_map(
        functools.partial(body, n),
        mesh=mesh,
        in_specs=(
            P(("dp", "tensor"), None),
            P(("dp", "tensor"), None),
            P(None, "tensor"),
            P("dp", "tensor"),
        ),
        out_specs=(P("dp", "tensor"), P(("dp", "tensor"), None), P("dp", "tensor")),
        check_vma=False,
    )
```

```python
import functools
import math
from types import SimpleNamespace

import jax
import jax.numpy as jnp
from jax import lax
from jax.experimental import pallas as pl
from jax.experimental.pallas import tpu as pltpu
from jax.sharding import PartitionSpec as P

MESH = pl.DeviceIdType.MESH
F32, BF16 = jnp.float32, jnp.bfloat16

SIZES = SimpleNamespace(H=2, Y=8, X=4, Z=6, C=2, B=16, R=48, F=640)
GROUP = 2


def permute_tiles(tiles, size, out_chunk_source):
    lane = lax.broadcasted_iota(jnp.int32, tiles[0].shape, 1)
    result = []
    for k in range(len(tiles)):
        runs = []
        for l in range(128):
            o = k * 128 + l
            src = out_chunk_source(o // size) * size + o % size
            key = (src // 128, (l - src) % 128)
            if runs and runs[-1][0] == key:
                runs[-1][2] = l + 1
            else:
                runs.append([key, l, l + 1])
        out = None
        for (tile, shift), lo, hi in runs:
            piece = tiles[tile]
            if shift:
                piece = pltpu.roll(piece, shift, 1)
            out = piece if out is None else jnp.where(lane >= lo, piece, out)
        result.append(out)
    return result


def kernel(
    n,
    mant_hbm, expo_hbm, w_hbm, ct_hbm,
    out_hbm, dx_out, dw_out,
    mant, expo, wp, wn, ct, xg, xq, gq, outv, prt, psib, dx_in, dx_send, dx_sum, acc, ysend, yrecv, tu, hsend, hrecv,
    loc, ag_s, ag_r, sib_s, sib_r, xs_s, xs_r, xb_s, xb_r, g_s, g_r, p_s, p_r, dx_s, dx_r, y_s, y_r,
    h_s, h_r, h_ready,
):
    H, Y, X, Z, C, B, R, F = n.H, n.Y, n.X, n.Z, n.C, n.B, n.R, n.F
    HY = H * Y
    D = HY * X * R
    Q = D // X
    NB = Z // GROUP
    BC = GROUP * B
    BT = C * BC
    T = NB * BT
    S = n.S
    SB = D // S
    FA = (F // 128 + 1) // 2 * 128

    dp = lax.axis_index("dp")
    tp = lax.axis_index("tensor")
    x = lax.rem(dp, X)
    y = lax.rem(dp // X, Y)
    h = dp // (X * Y)
    c = lax.rem(tp, C)
    z = tp // C
    plane = dp - x

    sib = (dp, tp + 1 - 2 * c)
    z_by = {(0, 1): (dp, tp + C), (0, 2): (dp, tp + 2 * C), (1, 1): (dp, tp - C), (1, 2): (dp, tp - 2 * C)}
    x_by = {k: (plane + lax.rem(x + k, X), tp) for k in (1, 2, 3)}
    y_by = {
        (way, k): ((h * Y + lax.rem(y + (k if way == 0 else Y - k), Y)) * X + x, tp) for way in (0, 1) for k in (1, 2)
    }
    h_by = (((1 - h) * Y + y) * X + x, tp)

    behind = (z, Z - 1 - z)
    ahead = (Z - 1 - z, z)

    def remote(src, dst, send, recv, device):
        return pltpu.make_async_remote_copy(
            src_ref=src, dst_ref=dst, send_sem=send, recv_sem=recv,
            device_id=device, device_id_type=MESH,
        )

    def arrived(dst, recv):
        remote(dst, dst, recv, recv, sib).wait_recv()

    def sent(src, send):
        remote(src, src, send, send, sib).wait_send()

    mant_in = pltpu.make_async_copy(mant_hbm, mant, loc.at[0])
    expo_in = pltpu.make_async_copy(expo_hbm, expo, loc.at[1])
    w_in = [pltpu.make_async_copy(w_hbm.at[:, k], wp.at[k], loc.at[2 + k]) for k in range(X)]
    ct_in = [pltpu.make_async_copy(ct_hbm.at[:, :, k], ct.at[:, k], loc.at[2 + X + k]) for k in range(C)]
    wn_in = pltpu.make_async_copy(w_hbm, wn, loc.at[2 + X + C])
    for copy in [mant_in, expo_in, *w_in, *ct_in, wn_in]:
        copy.start()

    barrier = pltpu.get_barrier_semaphore()

    def greet(device):
        pl.semaphore_signal(barrier, inc=1, device_id=device, device_id_type=MESH)

    for device in [sib, x_by[1], x_by[2], x_by[3], *y_by.values()]:
        greet(device)

    for way in (0, 1):
        for k in (1, 2):
            @pl.when(ahead[way] >= k)
            def _():
                greet(z_by[way, k])

    @pl.when(h == 0)
    def _():
        greet(h_by)

    def row(core, q):
        return (q // GROUP) * BT + core * BC + lax.rem(q, GROUP) * B

    def rows(core, q):
        return pl.ds(pl.multiple_of(row(core, q), B), B)

    def part_rows(core, b):
        return pl.ds(pl.multiple_of(b * BT + core * BC, BC), BC)

    mant_in.wait()
    expo_in.wait()
    factors = jnp.exp2(expo[...].astype(F32))
    tiles = [
        mant[:, pl.ds(128 * b, 128)].astype(F32) * factors[:, b : b + 1]
        for b in range(D // 128)
    ]
    for k, tile in enumerate(permute_tiles(tiles, R, lambda j: (j % HY) * X + j // HY)):
        xg[rows(c, z), pl.ds(128 * k, 128)] = tile.astype(BF16)

    count = 8 + h
    for way in (0, 1):
        count = count + jnp.minimum(ahead[way], 2)
    pl.semaphore_wait(barrier, count)

    @pl.when(h == 1)
    def _():
        pl.semaphore_signal(h_ready, inc=1, device_id=h_by, device_id_type=MESH)

    def block(way, far):
        return z - far if way == 0 else z + far

    def hop(way, far, k, sub):
        part = xg.at[rows(c, block(way, far)), pl.ds(sub * SB, SB)]
        at = far + k - 1
        return remote(part, part, ag_s.at[way, at, sub], ag_r.at[way, at, sub], z_by[way, k])

    def gathered(way, far, sub):
        arrived(xg.at[rows(c, block(way, far)), pl.ds(sub * SB, SB)], ag_r.at[way, far - 1, sub])

    def hops(far, act, sub, ways=(0, 1)):
        for way in ways:
            for k in (2, 1):
                if far + k < Z:
                    @pl.when((behind[way] >= far) & (ahead[way] >= k))
                    def _():
                        act(hop(way, far, k, sub))

    def spread_sibling(q):
        part = xg.at[rows(c, q), :]
        return remote(part, part, sib_s.at[q], sib_r.at[q], sib)

    def spread_x(q, k):
        to = lax.rem(x + k, X)
        at = pl.ds(pl.multiple_of(c * BC + lax.rem(q, GROUP) * B, B), B)
        return remote(
            xg.at[rows(c, q), pl.ds(pl.multiple_of(to * Q, Q), Q)],
            xq.at[q // GROUP, k, at, :],
            xs_s.at[k], xs_r.at[k, q // GROUP], x_by[k],
        )

    def spread(q):
        spread_sibling(q).start()
        for k in (2, 1, 3):
            spread_x(q, k).start()

    for sub in range(S):
        hops(0, lambda copy: copy.start(), sub)
    spread(z)

    def gather_step(far):
        for sub in range(S):
            for way in (0, 1):
                @pl.when(behind[way] >= far)
                def _():
                    gathered(way, far, sub)
                    if far % 2 == 0:
                        for k in (2, 1):
                            if far + k < Z:
                                @pl.when(ahead[way] >= k)
                                def _():
                                    hop(way, far, k, sub).start()

        for way in (0, 1):
            @pl.when(behind[way] >= far)
            def _():
                spread(block(way, far))

    def drain_gather():
        for far in range(0, Z, 2):
            for sub in range(S):
                hops(far, lambda copy: copy.wait_send(), sub)
        for q in range(Z):
            spread_sibling(q).wait_send()
        for k in (1, 2, 3):
            sent(xq.at[:, k, pl.ds(0, BC), :], xs_s.at[k])

    def batch(i):
        return jnp.where(z < Z // 2, i, NB - 1 - i)

    def g_part(b, k):
        return remote(gq.at[b, 0], gq.at[b, k], g_s.at[b, k], g_r.at[b, k], x_by[k])

    def forward(b):
        for i in range(GROUP):
            q = b * GROUP + i
            arrived(xg.at[rows(1 - c, q), :], sib_r.at[q])
        tokens = pl.ds(pl.multiple_of(b * BT, BT), BT)
        linear = jnp.dot(xg[tokens, pl.ds(0, Q)], wp[0].reshape(Q, F), preferred_element_type=F32)
        for k in range(1, X):
            linear = linear + jnp.dot(
                xg[tokens, pl.ds(k * Q, Q)], wp[k].reshape(Q, F), preferred_element_type=F32
            )
        sigmoid = jax.nn.sigmoid(linear)
        cot = ct[b].reshape(BT, F).astype(F32)
        gq[b, 0] = (cot * sigmoid * (1.0 + linear * (1.0 - sigmoid))).astype(BF16)
        for k in (2, 1, 3):
            g_part(b, k).start()
        outv[b] = (linear * sigmoid).astype(BF16).reshape(C, GROUP, B, F)
        xq[b, 0] = xg[tokens, pl.ds(pl.multiple_of(x * Q, Q), Q)]

    def x_sibling(b, k):
        part = xq.at[b, k, pl.ds(pl.multiple_of(c * BC, BC), BC), :]
        return remote(part, part, xb_s.at[b, k], xb_r.at[b, k], sib)

    def x_pass(b):
        for k in (1, 3, 2):
            arrived(xq.at[b, k, pl.ds(0, BC), :], xs_r.at[k, b])
            x_sibling(b, k).start()

    def dw_batch(b, first):
        for k in (1, 3, 2):
            x_sibling(b, k).wait_recv()
            g_part(b, k).wait_recv()
        part = lax.dot_general(
            xq[b].reshape(4 * BT, Q), gq[b].reshape(4 * BT, F),
            (((0,), (0,)), ((), ())), preferred_element_type=F32,
        )
        if first:
            acc[...] = part
        else:
            acc[...] += part

    order = [far for pair_of in ((2, 1), (4, 3), (6, 5)) for far in pair_of if far < Z]
    for copy in [*w_in, *ct_in]:
        copy.wait()
    for i in range(NB):
        for far in order[2 * i : 2 * i + 2] if i < NB - 1 else order[2 * i :]:
            gather_step(far)
        forward(batch(i))
        if i < NB - 1:
            x_pass(batch(i))

    out_back = [
        pltpu.make_async_copy(outv.at[:, k], out_hbm.at[:, :, k], loc.at[3 + X + C + k]) for k in range(C)
    ]
    for copy in out_back:
        copy.start()


    wn_in.wait()
    NC = X
    ND = D // NC

    def p_sibling(b, k):
        columns = pl.ds(k * ND, ND)
        return remote(
            prt.at[part_rows(1 - c, b), columns],
            psib.at[pl.ds(b * BC, BC), columns],
            p_s.at[b, k], p_r.at[b, k], sib,
        )

    grads = gq[:, 0].reshape(T, F)
    for k in range(NC):
        part = lax.dot_general(
            grads, wn[pl.ds(k * (HY // NC), HY // NC)].reshape(ND, F),
            (((1,), (1,)), ((), ())), preferred_element_type=F32,
        )
        prt[:, pl.ds(k * ND, ND)] = part.astype(BF16)
        for b in range(NB):
            p_sibling(b, k).start()

    def drain_g():
        for copy in out_back:
            copy.wait()
        for b in range(NB):
            for k in (1, 2, 3):
                x_sibling(b, k).wait_send()
                g_part(b, k).wait_send()
            for k in range(NC):
                p_sibling(b, k).wait_send()

    def pair(q):
        own = prt[rows(c, q), :].astype(F32)
        return own + psib[pl.ds(pl.multiple_of(q * B, B), B), :].astype(F32)

    def dx_to(way, far):
        return z + far if way == 0 else z - far

    def dx_hop(way, q, k):
        return remote(
            dx_send.at[way, q], dx_in.at[way, k - 1, q], dx_s.at[way, q], dx_r.at[way, k - 1, q], z_by[way, k]
        )

    def dx_add(way, q):
        for k in (1, 2):
            @pl.when(behind[way] >= k)
            def _():
                arrived(dx_in.at[way, k - 1, q], dx_r.at[way, k - 1, q])
                dx_sum[...] += dx_in[way, k - 1, q].astype(F32)

    def dx_step(far):
        if far >= Z:
            return
        for way in (0, 1):
            @pl.when(ahead[way] >= far)
            def _():
                q = dx_to(way, far)
                if far % 2 == 1:
                    dx_send[way, q] = pair(q).astype(BF16)
                else:
                    dx_sum[...] = pair(q)
                    dx_add(way, q)
                    dx_send[way, q] = dx_sum[...].astype(BF16)
                dx_hop(way, q, 2 - far % 2).start()

    def drain_dx():
        for far in range(1, Z):
            for way in (0, 1):
                @pl.when(ahead[way] >= far)
                def _():
                    dx_hop(way, dx_to(way, far), 2 - far % 2).wait_send()

    x_pass(batch(NB - 1))
    for i in range(NB - 1):
        dw_batch(batch(i), i == 0)
    for b in range(NB):
        for k in range(NC):
            p_sibling(b, k).wait_recv()
    for far in (5, 3, 1):
        dx_step(far)

    unit = [1 - h, h]
    share = (pl.ds(0, FA), pl.ds(FA, F - FA))

    def y_rows(i, to):
        return pl.ds(pl.multiple_of((unit[i] * Y + to) * R, R), R)

    def y_own(way, i, far):
        return acc[y_rows(i, lax.rem(y + (far if way == 0 else Y - far), Y)), :]

    def y_hop(way, i, part):
        src, dst = ysend.at[way, i, part], yrecv.at[way, i, part]
        if part == 1:
            src, dst = src.at[:, share[way]], dst.at[:, share[way]]
        return remote(src, dst, y_s.at[way, i, part], y_r.at[way, i, part], y_by[way, 1 + part % 2])

    def y_start(way, i, part):
        ysend[way, i, part] = y_own(way, i, (3, 4, 1)[part]).astype(BF16)
        y_hop(way, i, part).start()

    def y_relay(way, i):
        y_hop(way, i, 0).wait_recv()
        y_hop(way, i, 1).wait_recv()
        far = yrecv[way, i, 1, :, share[way]].astype(F32)
        none = jnp.zeros((R, F - far.shape[1]), F32)
        far = jnp.concatenate([far, none] if way == 0 else [none, far], axis=1)
        value = y_own(way, i, 2) + yrecv[way, i, 0].astype(F32) + far
        ysend[way, i, 3] = value.astype(BF16)
        y_hop(way, i, 3).start()

    def y_total(i):
        value = acc[y_rows(i, y), :]
        for part in (2, 3):
            for way in (0, 1):
                y_hop(way, i, part).wait_recv()
                value = value + yrecv[way, i, part].astype(F32)
        return value

    def drain_y():
        for way in (0, 1):
            for i in (0, 1):
                for part in range(4):
                    y_hop(way, i, part).wait_send()

    dw_batch(batch(NB - 1), NB == 1)


    for i in (0, 1):
        for part in (0, 1):
            for way in (0, 1):
                y_start(way, i, part)
    for i in (0, 1):
        for way in (0, 1):
            y_start(way, i, 2)
    dx_step(4)
    for i in (0, 1):
        for way in (0, 1):
            y_relay(way, i)
    dx_step(2)

    hsend[...] = y_total(0).astype(BF16)

    @pl.when(h == 0)
    def _():
        pl.semaphore_wait(h_ready, 1)

    across = remote(hsend, hrecv, h_s, h_r, h_by)
    across.start()
    tu[...] = y_total(1)

    dx_sum[...] = pair(z)
    for way in (0, 1):
        dx_add(way, z)
    dx_out[...] = dx_sum[...].astype(BF16)

    drain_gather()
    drain_g()
    drain_dx()
    drain_y()

    across.wait_recv()
    factor = 1.0 / math.sqrt(H * Y * X * T)
    dw_out[...] = (tu[...] + hrecv[...].astype(F32)) * factor
    across.wait_send()


def body(n, mantissas, exponents, weight, cotangent):
    H, Y, X, Z, C, B, R, F = n.H, n.Y, n.X, n.Z, n.C, n.B, n.R, n.F
    HY = H * Y
    D = HY * X * R
    Q, T, S = D // X, Z * B * C, n.S
    NB, BC = Z // GROUP, GROUP * B
    BT = C * BC
    anywhere = pl.BlockSpec(memory_space=pl.ANY)
    hbm = pl.BlockSpec(memory_space=pltpu.HBM)
    vmem = pl.BlockSpec(memory_space=pltpu.VMEM)
    dma = pltpu.SemaphoreType.DMA
    out, dx, dw = pl.pallas_call(
        functools.partial(kernel, n),
        out_shape=(
            jax.ShapeDtypeStruct((NB, GROUP, C, B, F), BF16),
            jax.ShapeDtypeStruct((B, D), BF16),
            jax.ShapeDtypeStruct((R, F), F32),
        ),
        in_specs=[hbm] * 4,
        out_specs=(anywhere, vmem, vmem),
        scratch_shapes=[
            pltpu.VMEM((B, D), BF16),
            pltpu.VMEM((B, D // 128), jnp.int32),
            pltpu.VMEM((X, HY, R, F), BF16),
            pltpu.VMEM((HY, X, R, F), BF16),
            pltpu.VMEM((NB, C, GROUP, B, F), BF16),
            pltpu.VMEM((T, D), BF16),
            pltpu.VMEM((NB, 4, BT, Q), BF16),
            pltpu.VMEM((NB, 4, BT, F), BF16),
            pltpu.VMEM((NB, C, GROUP, B, F), BF16),
            pltpu.VMEM((T, D), BF16),
            pltpu.VMEM((Z * B, D), BF16),
            pltpu.VMEM((2, 2, Z, B, D), BF16),
            pltpu.VMEM((2, Z, B, D), BF16),
            pltpu.VMEM((B, D), F32),
            pltpu.VMEM((Q, F), F32),
            pltpu.VMEM((2, 2, 4, R, F), BF16),
            pltpu.VMEM((2, 2, 4, R, F), BF16),
            pltpu.VMEM((R, F), F32),
            pltpu.VMEM((R, F), BF16),
            pltpu.VMEM((R, F), BF16),
            dma((3 + X + 2 * C,)),
            dma((2, Z, S)),
            dma((2, Z, S)),
            dma((Z,)),
            dma((Z,)),
            dma((4,)),
            dma((4, NB)),
            dma((NB, 4)),
            dma((NB, 4)),
            dma((NB, 4)),
            dma((NB, 4)),
            dma((NB, X)),
            dma((NB, X)),
            dma((2, Z)),
            dma((2, 2, Z)),
            dma((2, 2, 4)),
            dma((2, 2, 4)),
            dma,
            dma,
            pltpu.SemaphoreType.REGULAR,
        ],
        compiler_params=pltpu.CompilerParams(
            collective_id=0, has_side_effects=True, vmem_limit_bytes=62 * 1024 * 1024
        ),
        cost_estimate=pl.CostEstimate(
            flops=6 * T * D * F, bytes_accessed=4 * D * F, transcendentals=T * F
        ),
    )(
        mantissas,
        exponents,
        weight.reshape(HY, X, R, F),
        cotangent.reshape(NB, GROUP, C, B, F),
    )
    return out.reshape(T, F), dx, dw


def solution(mesh, sizes=SIZES):
    n = SimpleNamespace(**vars(sizes), S=2)
    return jax.shard_map(
        functools.partial(body, n),
        mesh=mesh,
        in_specs=(
            P(("dp", "tensor"), None),
            P(("dp", "tensor"), None),
            P(None, "tensor"),
            P("dp", "tensor"),
        ),
        out_specs=(P("dp", "tensor"), P(("dp", "tensor"), None), P("dp", "tensor")),
        check_vma=False,
    )
```

```python
import functools
import math
from types import SimpleNamespace

import jax
import jax.numpy as jnp
from jax import lax
from jax.experimental import pallas as pl
from jax.experimental.pallas import tpu as pltpu
from jax.sharding import PartitionSpec as P

MESH = pl.DeviceIdType.MESH
F32, BF16 = jnp.float32, jnp.bfloat16

SIZES = SimpleNamespace(H=2, Y=8, X=4, Z=6, C=2, B=16, R=48, F=640)
GROUP = 2


def permute_tiles(tiles, size, out_chunk_source):
    lane = lax.broadcasted_iota(jnp.int32, tiles[0].shape, 1)
    result = []
    for k in range(len(tiles)):
        runs = []
        for l in range(128):
            o = k * 128 + l
            src = out_chunk_source(o // size) * size + o % size
            key = (src // 128, (l - src) % 128)
            if runs and runs[-1][0] == key:
                runs[-1][2] = l + 1
            else:
                runs.append([key, l, l + 1])
        out = None
        for (tile, shift), lo, hi in runs:
            piece = tiles[tile]
            if shift:
                piece = pltpu.roll(piece, shift, 1)
            out = piece if out is None else jnp.where(lane >= lo, piece, out)
        result.append(out)
    return result


def kernel(
    n,
    mant_hbm, expo_hbm, w_hbm, ct_hbm,
    out_hbm, dx_out, dw_out,
    mant, expo, wp, wn, ct, xg, xq, gq, outv, prt, psib, dx_in, dx_send, dx_sum, acc, ysend, yrecv, tu, hsend, hrecv,
    loc, ag_s, ag_r, sib_s, sib_r, xs_s, xs_r, xb_s, xb_r, g_s, g_r, p_s, p_r, dx_s, dx_r, y_s, y_r,
    h_s, h_r, h_ready,
):
    H, Y, X, Z, C, B, R, F = n.H, n.Y, n.X, n.Z, n.C, n.B, n.R, n.F
    HY = H * Y
    D = HY * X * R
    Q = D // X
    NB = Z // GROUP
    BC = GROUP * B
    BT = C * BC
    T = NB * BT
    S = n.S
    SB = D // S
    FA = (F // 128 + 1) // 2 * 128

    dp = lax.axis_index("dp")
    tp = lax.axis_index("tensor")
    x = lax.rem(dp, X)
    y = lax.rem(dp // X, Y)
    h = dp // (X * Y)
    c = lax.rem(tp, C)
    z = tp // C
    plane = dp - x

    sib = (dp, tp + 1 - 2 * c)
    z_by = {(0, 1): (dp, tp + C), (0, 2): (dp, tp + 2 * C), (1, 1): (dp, tp - C), (1, 2): (dp, tp - 2 * C)}
    x_by = {k: (plane + lax.rem(x + k, X), tp) for k in (1, 2, 3)}
    y_by = {
        (way, k): ((h * Y + lax.rem(y + (k if way == 0 else Y - k), Y)) * X + x, tp) for way in (0, 1) for k in (1, 2)
    }
    h_by = (((1 - h) * Y + y) * X + x, tp)

    behind = (z, Z - 1 - z)
    ahead = (Z - 1 - z, z)

    def remote(src, dst, send, recv, device):
        return pltpu.make_async_remote_copy(
            src_ref=src, dst_ref=dst, send_sem=send, recv_sem=recv,
            device_id=device, device_id_type=MESH,
        )

    def arrived(dst, recv):
        remote(dst, dst, recv, recv, sib).wait_recv()

    def sent(src, send):
        remote(src, src, send, send, sib).wait_send()

    mant_in = pltpu.make_async_copy(mant_hbm, mant, loc.at[0])
    expo_in = pltpu.make_async_copy(expo_hbm, expo, loc.at[1])
    w_in = [pltpu.make_async_copy(w_hbm.at[:, k], wp.at[k], loc.at[2 + k]) for k in range(X)]
    ct_in = [pltpu.make_async_copy(ct_hbm.at[:, :, k], ct.at[:, k], loc.at[2 + X + k]) for k in range(C)]
    wn_in = pltpu.make_async_copy(w_hbm, wn, loc.at[2 + X + C])
    for copy in [mant_in, expo_in, *w_in, *ct_in, wn_in]:
        copy.start()

    barrier = pltpu.get_barrier_semaphore()

    def greet(device):
        pl.semaphore_signal(barrier, inc=1, device_id=device, device_id_type=MESH)

    for device in [sib, x_by[1], x_by[2], x_by[3], *y_by.values()]:
        greet(device)

    for way in (0, 1):
        for k in (1, 2):
            @pl.when(ahead[way] >= k)
            def _():
                greet(z_by[way, k])

    @pl.when(h == 0)
    def _():
        greet(h_by)

    def row(core, q):
        return (q // GROUP) * BT + core * BC + lax.rem(q, GROUP) * B

    def rows(core, q):
        return pl.ds(pl.multiple_of(row(core, q), B), B)

    def part_rows(core, b):
        return pl.ds(pl.multiple_of(b * BT + core * BC, BC), BC)

    mant_in.wait()
    expo_in.wait()
    factors = jnp.exp2(expo[...].astype(F32))
    tiles = [
        mant[:, pl.ds(128 * b, 128)].astype(F32) * factors[:, b : b + 1]
        for b in range(D // 128)
    ]
    for k, tile in enumerate(permute_tiles(tiles, R, lambda j: (j % HY) * X + j // HY)):
        xg[rows(c, z), pl.ds(128 * k, 128)] = tile.astype(BF16)

    count = 8 + h
    for way in (0, 1):
        count = count + jnp.minimum(ahead[way], 2)
    pl.semaphore_wait(barrier, count)

    @pl.when(h == 1)
    def _():
        pl.semaphore_signal(h_ready, inc=1, device_id=h_by, device_id_type=MESH)

    def block(way, far):
        return z - far if way == 0 else z + far

    def hop(way, far, k, sub):
        part = xg.at[rows(c, block(way, far)), pl.ds(sub * SB, SB)]
        at = far + k - 1
        return remote(part, part, ag_s.at[way, at, sub], ag_r.at[way, at, sub], z_by[way, k])

    def gathered(way, far, sub):
        arrived(xg.at[rows(c, block(way, far)), pl.ds(sub * SB, SB)], ag_r.at[way, far - 1, sub])

    def hops(far, act, sub, ways=(0, 1)):
        for way in ways:
            for k in (2, 1):
                if far + k < Z:
                    @pl.when((behind[way] >= far) & (ahead[way] >= k))
                    def _():
                        act(hop(way, far, k, sub))

    def spread_sibling(q):
        part = xg.at[rows(c, q), :]
        return remote(part, part, sib_s.at[q], sib_r.at[q], sib)

    def spread_x(q, k):
        to = lax.rem(x + k, X)
        at = pl.ds(pl.multiple_of(c * BC + lax.rem(q, GROUP) * B, B), B)
        return remote(
            xg.at[rows(c, q), pl.ds(pl.multiple_of(to * Q, Q), Q)],
            xq.at[q // GROUP, k, at, :],
            xs_s.at[k], xs_r.at[k, q // GROUP], x_by[k],
        )

    def spread(q):
        spread_sibling(q).start()
        for k in (2, 1, 3):
            spread_x(q, k).start()

    for sub in range(S):
        hops(0, lambda copy: copy.start(), sub)
    spread(z)

    def gather_step(far):
        for sub in range(S):
            for way in (0, 1):
                @pl.when(behind[way] >= far)
                def _():
                    gathered(way, far, sub)
                    if far % 2 == 0:
                        for k in (2, 1):
                            if far + k < Z:
                                @pl.when(ahead[way] >= k)
                                def _():
                                    hop(way, far, k, sub).start()

        for way in (0, 1):
            @pl.when(behind[way] >= far)
            def _():
                spread(block(way, far))

    def drain_gather():
        for far in range(0, Z, 2):
            for sub in range(S):
                hops(far, lambda copy: copy.wait_send(), sub)
        for q in range(Z):
            spread_sibling(q).wait_send()
        for k in (1, 2, 3):
            sent(xq.at[:, k, pl.ds(0, BC), :], xs_s.at[k])

    def batch(i):
        return jnp.where(z < Z // 2, i, NB - 1 - i)

    def g_part(b, k):
        return remote(gq.at[b, 0], gq.at[b, k], g_s.at[b, k], g_r.at[b, k], x_by[k])

    def forward(b):
        for i in range(GROUP):
            q = b * GROUP + i
            arrived(xg.at[rows(1 - c, q), :], sib_r.at[q])
        tokens = pl.ds(pl.multiple_of(b * BT, BT), BT)
        linear = jnp.dot(xg[tokens, pl.ds(0, Q)], wp[0].reshape(Q, F), preferred_element_type=F32)
        for k in range(1, X):
            linear = linear + jnp.dot(
                xg[tokens, pl.ds(k * Q, Q)], wp[k].reshape(Q, F), preferred_element_type=F32
            )
        sigmoid = jax.nn.sigmoid(linear)
        cot = ct[b].reshape(BT, F).astype(F32)
        gq[b, 0] = (cot * sigmoid * (1.0 + linear * (1.0 - sigmoid))).astype(BF16)
        for k in (2, 1, 3):
            g_part(b, k).start()
        outv[b] = (linear * sigmoid).astype(BF16).reshape(C, GROUP, B, F)
        xq[b, 0] = xg[tokens, pl.ds(pl.multiple_of(x * Q, Q), Q)]

    def x_sibling(b, k):
        part = xq.at[b, k, pl.ds(pl.multiple_of(c * BC, BC), BC), :]
        return remote(part, part, xb_s.at[b, k], xb_r.at[b, k], sib)

    def x_pass(b):
        for k in (1, 3, 2):
            arrived(xq.at[b, k, pl.ds(0, BC), :], xs_r.at[k, b])
            x_sibling(b, k).start()

    def dw_batch(b, first):
        for k in (1, 3, 2):
            x_sibling(b, k).wait_recv()
            g_part(b, k).wait_recv()
        part = lax.dot_general(
            xq[b].reshape(4 * BT, Q), gq[b].reshape(4 * BT, F),
            (((0,), (0,)), ((), ())), preferred_element_type=F32,
        )
        if first:
            acc[...] = part
        else:
            acc[...] += part

    order = [far for pair_of in ((2, 1), (4, 3), (6, 5)) for far in pair_of if far < Z]
    for copy in [*w_in, *ct_in]:
        copy.wait()
    for i in range(NB):
        for far in order[2 * i : 2 * i + 2] if i < NB - 1 else order[2 * i :]:
            gather_step(far)
        forward(batch(i))
        if i < NB - 1:
            x_pass(batch(i))

    out_back = [
        pltpu.make_async_copy(outv.at[:, k], out_hbm.at[:, :, k], loc.at[3 + X + C + k]) for k in range(C)
    ]
    for copy in out_back:
        copy.start()


    wn_in.wait()
    NC = X
    ND = D // NC

    def p_sibling(b, k):
        columns = pl.ds(k * ND, ND)
        return remote(
            prt.at[part_rows(1 - c, b), columns],
            psib.at[pl.ds(b * BC, BC), columns],
            p_s.at[b, k], p_r.at[b, k], sib,
        )

    grads = gq[:, 0].reshape(T, F)
    for k in range(NC):
        part = lax.dot_general(
            grads, wn[pl.ds(k * (HY // NC), HY // NC)].reshape(ND, F),
            (((1,), (1,)), ((), ())), preferred_element_type=F32,
        )
        prt[:, pl.ds(k * ND, ND)] = part.astype(BF16)
        for b in range(NB):
            p_sibling(b, k).start()

    def drain_g():
        for copy in out_back:
            copy.wait()
        for b in range(NB):
            for k in (1, 2, 3):
                x_sibling(b, k).wait_send()
                g_part(b, k).wait_send()
            for k in range(NC):
                p_sibling(b, k).wait_send()

    def pair(q):
        own = prt[rows(c, q), :].astype(F32)
        return own + psib[pl.ds(pl.multiple_of(q * B, B), B), :].astype(F32)

    def dx_to(way, far):
        return z + far if way == 0 else z - far

    def dx_hop(way, q, k):
        return remote(
            dx_send.at[way, q], dx_in.at[way, k - 1, q], dx_s.at[way, q], dx_r.at[way, k - 1, q], z_by[way, k]
        )

    def dx_add(way, q):
        for k in (1, 2):
            @pl.when(behind[way] >= k)
            def _():
                arrived(dx_in.at[way, k - 1, q], dx_r.at[way, k - 1, q])
                dx_sum[...] += dx_in[way, k - 1, q].astype(F32)

    def dx_step(far):
        if far >= Z:
            return
        for way in (0, 1):
            @pl.when(ahead[way] >= far)
            def _():
                q = dx_to(way, far)
                if far % 2 == 1:
                    dx_send[way, q] = pair(q).astype(BF16)
                else:
                    dx_sum[...] = pair(q)
                    dx_add(way, q)
                    dx_send[way, q] = dx_sum[...].astype(BF16)
                dx_hop(way, q, 2 - far % 2).start()

    def drain_dx():
        for far in range(1, Z):
            for way in (0, 1):
                @pl.when(ahead[way] >= far)
                def _():
                    dx_hop(way, dx_to(way, far), 2 - far % 2).wait_send()

    x_pass(batch(NB - 1))
    for i in range(NB - 1):
        dw_batch(batch(i), i == 0)
    for b in range(NB):
        for k in range(NC):
            p_sibling(b, k).wait_recv()
    for far in (5, 3, 1):
        dx_step(far)

    unit = [1 - h, h]
    share = (pl.ds(0, FA), pl.ds(FA, F - FA))

    def y_rows(i, to):
        return pl.ds(pl.multiple_of((unit[i] * Y + to) * R, R), R)

    def y_own(way, i, far):
        return acc[y_rows(i, lax.rem(y + (far if way == 0 else Y - far), Y)), :]

    def y_hop(way, i, part):
        src, dst = ysend.at[way, i, part], yrecv.at[way, i, part]
        if part == 1:
            src, dst = src.at[:, share[way]], dst.at[:, share[way]]
        return remote(src, dst, y_s.at[way, i, part], y_r.at[way, i, part], y_by[way, 1 + part % 2])

    def y_start(way, i, part):
        ysend[way, i, part] = y_own(way, i, (3, 4, 1)[part]).astype(BF16)
        y_hop(way, i, part).start()

    def y_relay(way, i):
        y_hop(way, i, 0).wait_recv()
        y_hop(way, i, 1).wait_recv()
        far = yrecv[way, i, 1, :, share[way]].astype(F32)
        none = jnp.zeros((R, F - far.shape[1]), F32)
        far = jnp.concatenate([far, none] if way == 0 else [none, far], axis=1)
        value = y_own(way, i, 2) + yrecv[way, i, 0].astype(F32) + far
        ysend[way, i, 3] = value.astype(BF16)
        y_hop(way, i, 3).start()

    def y_total(i):
        value = acc[y_rows(i, y), :]
        for part in (2, 3):
            for way in (0, 1):
                y_hop(way, i, part).wait_recv()
                value = value + yrecv[way, i, part].astype(F32)
        return value

    def drain_y():
        for way in (0, 1):
            for i in (0, 1):
                for part in range(4):
                    y_hop(way, i, part).wait_send()

    dw_batch(batch(NB - 1), NB == 1)


    for i in (0, 1):
        for part in (0, 1):
            for way in (0, 1):
                y_start(way, i, part)
    for i in (0, 1):
        for way in (0, 1):
            y_start(way, i, 2)
    dx_step(4)
    for i in (0, 1):
        for way in (0, 1):
            y_relay(way, i)
    dx_step(2)

    hsend[...] = y_total(0).astype(BF16)

    @pl.when(h == 0)
    def _():
        pl.semaphore_wait(h_ready, 1)

    across = remote(hsend, hrecv, h_s, h_r, h_by)
    across.start()
    tu[...] = y_total(1)

    dx_sum[...] = pair(z)
    for way in (0, 1):
        dx_add(way, z)
    dx_out[...] = dx_sum[...].astype(BF16)

    drain_gather()
    drain_g()
    drain_dx()
    drain_y()

    across.wait_recv()
    factor = 1.0 / math.sqrt(H * Y * X * T)
    dw_out[...] = (tu[...] + hrecv[...].astype(F32)) * factor
    across.wait_send()


def body(n, mantissas, exponents, weight, cotangent):
    H, Y, X, Z, C, B, R, F = n.H, n.Y, n.X, n.Z, n.C, n.B, n.R, n.F
    HY = H * Y
    D = HY * X * R
    Q, T, S = D // X, Z * B * C, n.S
    NB, BC = Z // GROUP, GROUP * B
    BT = C * BC
    anywhere = pl.BlockSpec(memory_space=pl.ANY)
    hbm = pl.BlockSpec(memory_space=pltpu.HBM)
    vmem = pl.BlockSpec(memory_space=pltpu.VMEM)
    dma = pltpu.SemaphoreType.DMA
    out, dx, dw = pl.pallas_call(
        functools.partial(kernel, n),
        out_shape=(
            jax.ShapeDtypeStruct((NB, GROUP, C, B, F), BF16),
            jax.ShapeDtypeStruct((B, D), BF16),
            jax.ShapeDtypeStruct((R, F), F32),
        ),
        in_specs=[hbm] * 4,
        out_specs=(anywhere, vmem, vmem),
        scratch_shapes=[
            pltpu.VMEM((B, D), BF16),
            pltpu.VMEM((B, D // 128), jnp.int32),
            pltpu.VMEM((X, HY, R, F), BF16),
            pltpu.VMEM((HY, X, R, F), BF16),
            pltpu.VMEM((NB, C, GROUP, B, F), BF16),
            pltpu.VMEM((T, D), BF16),
            pltpu.VMEM((NB, 4, BT, Q), BF16),
            pltpu.VMEM((NB, 4, BT, F), BF16),
            pltpu.VMEM((NB, C, GROUP, B, F), BF16),
            pltpu.VMEM((T, D), BF16),
            pltpu.VMEM((Z * B, D), BF16),
            pltpu.VMEM((2, 2, Z, B, D), BF16),
            pltpu.VMEM((2, Z, B, D), BF16),
            pltpu.VMEM((B, D), F32),
            pltpu.VMEM((Q, F), F32),
            pltpu.VMEM((2, 2, 4, R, F), BF16),
            pltpu.VMEM((2, 2, 4, R, F), BF16),
            pltpu.VMEM((R, F), F32),
            pltpu.VMEM((R, F), BF16),
            pltpu.VMEM((R, F), BF16),
            dma((3 + X + 2 * C,)),
            dma((2, Z, S)),
            dma((2, Z, S)),
            dma((Z,)),
            dma((Z,)),
            dma((4,)),
            dma((4, NB)),
            dma((NB, 4)),
            dma((NB, 4)),
            dma((NB, 4)),
            dma((NB, 4)),
            dma((NB, X)),
            dma((NB, X)),
            dma((2, Z)),
            dma((2, 2, Z)),
            dma((2, 2, 4)),
            dma((2, 2, 4)),
            dma,
            dma,
            pltpu.SemaphoreType.REGULAR,
        ],
        compiler_params=pltpu.CompilerParams(
            collective_id=0, has_side_effects=True, vmem_limit_bytes=50 * 1024 * 1024
        ),
        cost_estimate=pl.CostEstimate(
            flops=6 * T * D * F, bytes_accessed=4 * D * F, transcendentals=T * F
        ),
    )(
        *(
            pltpu.with_memory_space_constraint(a, pltpu.HBM)
            for a in (
                mantissas,
                exponents,
                weight.reshape(HY, X, R, F),
                cotangent.reshape(NB, GROUP, C, B, F),
            )
        ),
    )
    return out.reshape(T, F), dx, dw


def solution(mesh, sizes=SIZES):
    n = SimpleNamespace(**vars(sizes), S=2)
    return jax.shard_map(
        functools.partial(body, n),
        mesh=mesh,
        in_specs=(
            P(("dp", "tensor"), None),
            P(("dp", "tensor"), None),
            P(None, "tensor"),
            P("dp", "tensor"),
        ),
        out_specs=(P("dp", "tensor"), P(("dp", "tensor"), None), P("dp", "tensor")),
        check_vma=False,
    )
```

```python
import functools
import math
from types import SimpleNamespace

import jax
import jax.numpy as jnp
from jax import lax
from jax.experimental import pallas as pl
from jax.experimental.pallas import tpu as pltpu
from jax.sharding import PartitionSpec as P

MESH = pl.DeviceIdType.MESH
F32, BF16 = jnp.float32, jnp.bfloat16

SIZES = SimpleNamespace(H=2, Y=8, X=4, Z=6, C=2, B=16, R=48, F=640)
GROUP = 2


def permute_tiles(tiles, size, out_chunk_source):
    lane = lax.broadcasted_iota(jnp.int32, tiles[0].shape, 1)
    result = []
    for k in range(len(tiles)):
        runs = []
        for l in range(128):
            o = k * 128 + l
            src = out_chunk_source(o // size) * size + o % size
            key = (src // 128, (l - src) % 128)
            if runs and runs[-1][0] == key:
                runs[-1][2] = l + 1
            else:
                runs.append([key, l, l + 1])
        out = None
        for (tile, shift), lo, hi in runs:
            piece = tiles[tile]
            if shift:
                piece = pltpu.roll(piece, shift, 1)
            out = piece if out is None else jnp.where(lane >= lo, piece, out)
        result.append(out)
    return result


def kernel(
    n,
    mant_hbm, expo_hbm, w_hbm, ct_hbm,
    out_hbm, dx_out, dw_out,
    mant, expo, wp, wn, ct, xg, xq, gq, outv, prt, psib, dx_in, dx_send, dx_sum, acc, ysend, yrecv, tu, hsend, hrecv,
    loc, ag_s, ag_r, sib_s, sib_r, xs_s, xs_r, xb_s, xb_r, g_s, g_r, p_s, p_r, dx_s, dx_r, y_s, y_r,
    h_s, h_r, h_ready,
):
    H, Y, X, Z, C, B, R, F = n.H, n.Y, n.X, n.Z, n.C, n.B, n.R, n.F
    HY = H * Y
    D = HY * X * R
    Q = D // X
    NB = Z // GROUP
    BC = GROUP * B
    BT = C * BC
    T = NB * BT
    S = n.S
    SB = D // S
    FA = (F // 128 + 1) // 2 * 128

    dp = lax.axis_index("dp")
    tp = lax.axis_index("tensor")
    x = lax.rem(dp, X)
    y = lax.rem(dp // X, Y)
    h = dp // (X * Y)
    c = lax.rem(tp, C)
    z = tp // C
    plane = dp - x

    sib = (dp, tp + 1 - 2 * c)
    z_by = {(0, 1): (dp, tp + C), (0, 2): (dp, tp + 2 * C), (1, 1): (dp, tp - C), (1, 2): (dp, tp - 2 * C)}
    x_by = {k: (plane + lax.rem(x + k, X), tp) for k in (1, 2, 3)}
    y_by = {
        (way, k): ((h * Y + lax.rem(y + (k if way == 0 else Y - k), Y)) * X + x, tp) for way in (0, 1) for k in (1, 2)
    }
    h_by = (((1 - h) * Y + y) * X + x, tp)

    behind = (z, Z - 1 - z)
    ahead = (Z - 1 - z, z)

    def remote(src, dst, send, recv, device):
        return pltpu.make_async_remote_copy(
            src_ref=src, dst_ref=dst, send_sem=send, recv_sem=recv,
            device_id=device, device_id_type=MESH,
        )

    def arrived(dst, recv):
        remote(dst, dst, recv, recv, sib).wait_recv()

    def sent(src, send):
        remote(src, src, send, send, sib).wait_send()

    mant_in = pltpu.make_async_copy(mant_hbm, mant, loc.at[0])
    expo_in = pltpu.make_async_copy(expo_hbm, expo, loc.at[1])
    w_in = [pltpu.make_async_copy(w_hbm.at[:, k], wp.at[k], loc.at[2 + k]) for k in range(X)]
    ct_in = [pltpu.make_async_copy(ct_hbm.at[:, :, k], ct.at[:, k], loc.at[2 + X + k]) for k in range(C)]
    wn_in = pltpu.make_async_copy(w_hbm, wn, loc.at[2 + X + C])
    for copy in [mant_in, expo_in, *w_in, *ct_in, wn_in]:
        copy.start()

    barrier = pltpu.get_barrier_semaphore()

    def greet(device):
        pl.semaphore_signal(barrier, inc=1, device_id=device, device_id_type=MESH)

    for device in [sib, x_by[1], x_by[2], x_by[3], *y_by.values()]:
        greet(device)

    for way in (0, 1):
        for k in (1, 2):
            @pl.when(ahead[way] >= k)
            def _():
                greet(z_by[way, k])

    @pl.when(h == 0)
    def _():
        greet(h_by)

    def row(core, q):
        return (q // GROUP) * BT + core * BC + lax.rem(q, GROUP) * B

    def rows(core, q):
        return pl.ds(pl.multiple_of(row(core, q), B), B)

    def part_rows(core, b):
        return pl.ds(pl.multiple_of(b * BT + core * BC, BC), BC)

    mant_in.wait()
    expo_in.wait()
    factors = jnp.exp2(expo[...].astype(F32))
    tiles = [
        mant[:, pl.ds(128 * b, 128)].astype(F32) * factors[:, b : b + 1]
        for b in range(D // 128)
    ]
    for k, tile in enumerate(permute_tiles(tiles, R, lambda j: (j % HY) * X + j // HY)):
        xg[rows(c, z), pl.ds(128 * k, 128)] = tile.astype(BF16)

    count = 8 + h
    for way in (0, 1):
        count = count + jnp.minimum(ahead[way], 2)
    pl.semaphore_wait(barrier, count)

    @pl.when(h == 1)
    def _():
        pl.semaphore_signal(h_ready, inc=1, device_id=h_by, device_id_type=MESH)

    def block(way, far):
        return z - far if way == 0 else z + far

    def hop(way, far, k, sub):
        part = xg.at[rows(c, block(way, far)), pl.ds(sub * SB, SB)]
        at = far + k - 1
        return remote(part, part, ag_s.at[way, at, sub], ag_r.at[way, at, sub], z_by[way, k])

    def gathered(way, far, sub):
        arrived(xg.at[rows(c, block(way, far)), pl.ds(sub * SB, SB)], ag_r.at[way, far - 1, sub])

    def hops(far, act, sub, ways=(0, 1)):
        for way in ways:
            for k in (2, 1):
                if far + k < Z:
                    @pl.when((behind[way] >= far) & (ahead[way] >= k))
                    def _():
                        act(hop(way, far, k, sub))

    def spread_sibling(q):
        part = xg.at[rows(c, q), :]
        return remote(part, part, sib_s.at[q], sib_r.at[q], sib)

    def spread_x(q, k):
        to = lax.rem(x + k, X)
        at = pl.ds(pl.multiple_of(c * BC + lax.rem(q, GROUP) * B, B), B)
        return remote(
            xg.at[rows(c, q), pl.ds(pl.multiple_of(to * Q, Q), Q)],
            xq.at[q // GROUP, k, at, :],
            xs_s.at[k], xs_r.at[k, q // GROUP], x_by[k],
        )

    def spread(q):
        spread_sibling(q).start()
        for k in (2, 1, 3):
            spread_x(q, k).start()

    for sub in range(S):
        hops(0, lambda copy: copy.start(), sub)
    spread(z)

    def gather_step(far):
        for sub in range(S):
            for way in (0, 1):
                @pl.when(behind[way] >= far)
                def _():
                    gathered(way, far, sub)
                    if far % 2 == 0:
                        for k in (2, 1):
                            if far + k < Z:
                                @pl.when(ahead[way] >= k)
                                def _():
                                    hop(way, far, k, sub).start()

        for way in (0, 1):
            @pl.when(behind[way] >= far)
            def _():
                spread(block(way, far))

    def drain_gather():
        for far in range(0, Z, 2):
            for sub in range(S):
                hops(far, lambda copy: copy.wait_send(), sub)
        for q in range(Z):
            spread_sibling(q).wait_send()
        for k in (1, 2, 3):
            sent(xq.at[:, k, pl.ds(0, BC), :], xs_s.at[k])

    def batch(i):
        return jnp.where(z < Z // 2, i, NB - 1 - i)

    def g_part(b, k):
        return remote(gq.at[b, 0], gq.at[b, k], g_s.at[b, k], g_r.at[b, k], x_by[k])

    def forward(b):
        for i in range(GROUP):
            q = b * GROUP + i
            arrived(xg.at[rows(1 - c, q), :], sib_r.at[q])
        tokens = pl.ds(pl.multiple_of(b * BT, BT), BT)
        linear = jnp.dot(xg[tokens, pl.ds(0, Q)], wp[0].reshape(Q, F), preferred_element_type=F32)
        for k in range(1, X):
            linear = linear + jnp.dot(
                xg[tokens, pl.ds(k * Q, Q)], wp[k].reshape(Q, F), preferred_element_type=F32
            )
        sigmoid = jax.nn.sigmoid(linear)
        cot = ct[b].reshape(BT, F).astype(F32)
        gq[b, 0] = (cot * sigmoid * (1.0 + linear * (1.0 - sigmoid))).astype(BF16)
        for k in (2, 1, 3):
            g_part(b, k).start()
        outv[b] = (linear * sigmoid).astype(BF16).reshape(C, GROUP, B, F)
        xq[b, 0] = xg[tokens, pl.ds(pl.multiple_of(x * Q, Q), Q)]

    def x_sibling(b, k):
        part = xq.at[b, k, pl.ds(pl.multiple_of(c * BC, BC), BC), :]
        return remote(part, part, xb_s.at[b, k], xb_r.at[b, k], sib)

    def x_pass(b):
        for k in (1, 3, 2):
            arrived(xq.at[b, k, pl.ds(0, BC), :], xs_r.at[k, b])
            x_sibling(b, k).start()

    def dw_batch(b, first):
        for k in (1, 3, 2):
            x_sibling(b, k).wait_recv()
            g_part(b, k).wait_recv()
        part = lax.dot_general(
            xq[b].reshape(4 * BT, Q), gq[b].reshape(4 * BT, F),
            (((0,), (0,)), ((), ())), preferred_element_type=F32,
        )
        if first:
            acc[...] = part
        else:
            acc[...] += part

    order = [far for pair_of in ((2, 1), (4, 3), (6, 5)) for far in pair_of if far < Z]
    for copy in [*w_in, *ct_in]:
        copy.wait()
    for i in range(NB):
        for far in order[2 * i : 2 * i + 2] if i < NB - 1 else order[2 * i :]:
            gather_step(far)
        forward(batch(i))
        if i < NB - 1:
            x_pass(batch(i))

    out_back = [
        pltpu.make_async_copy(outv.at[:, k], out_hbm.at[:, :, k], loc.at[3 + X + C + k]) for k in range(C)
    ]
    for copy in out_back:
        copy.start()


    wn_in.wait()
    NC = X
    ND = D // NC

    def p_sibling(b, k):
        columns = pl.ds(k * ND, ND)
        return remote(
            prt.at[part_rows(1 - c, b), columns],
            psib.at[pl.ds(b * BC, BC), columns],
            p_s.at[b, k], p_r.at[b, k], sib,
        )

    grads = gq[:, 0].reshape(T, F)
    for k in range(NC):
        part = lax.dot_general(
            grads, wn[pl.ds(k * (HY // NC), HY // NC)].reshape(ND, F),
            (((1,), (1,)), ((), ())), preferred_element_type=F32,
        )
        prt[:, pl.ds(k * ND, ND)] = part.astype(BF16)
        for b in range(NB):
            p_sibling(b, k).start()

    def drain_g():
        for copy in out_back:
            copy.wait()
        for b in range(NB):
            for k in (1, 2, 3):
                x_sibling(b, k).wait_send()
                g_part(b, k).wait_send()
            for k in range(NC):
                p_sibling(b, k).wait_send()

    def pair(q):
        own = prt[rows(c, q), :].astype(F32)
        return own + psib[pl.ds(pl.multiple_of(q * B, B), B), :].astype(F32)

    def dx_to(way, far):
        return z + far if way == 0 else z - far

    def dx_hop(way, q, k):
        return remote(
            dx_send.at[way, q], dx_in.at[way, k - 1, q], dx_s.at[way, q], dx_r.at[way, k - 1, q], z_by[way, k]
        )

    def dx_add(way, q):
        for k in (1, 2):
            @pl.when(behind[way] >= k)
            def _():
                arrived(dx_in.at[way, k - 1, q], dx_r.at[way, k - 1, q])
                dx_sum[...] += dx_in[way, k - 1, q].astype(F32)

    def dx_step(far):
        if far >= Z:
            return
        for way in (0, 1):
            @pl.when(ahead[way] >= far)
            def _():
                q = dx_to(way, far)
                if far % 2 == 1:
                    dx_send[way, q] = pair(q).astype(BF16)
                else:
                    dx_sum[...] = pair(q)
                    dx_add(way, q)
                    dx_send[way, q] = dx_sum[...].astype(BF16)
                dx_hop(way, q, 2 - far % 2).start()

    def drain_dx():
        for far in range(1, Z):
            for way in (0, 1):
                @pl.when(ahead[way] >= far)
                def _():
                    dx_hop(way, dx_to(way, far), 2 - far % 2).wait_send()

    x_pass(batch(NB - 1))
    for i in range(NB - 1):
        dw_batch(batch(i), i == 0)
    for b in range(NB):
        for k in range(NC):
            p_sibling(b, k).wait_recv()
    for far in (5, 3, 1):
        dx_step(far)

    unit = [1 - h, h]
    share = (pl.ds(0, FA), pl.ds(FA, F - FA))

    def y_rows(i, to):
        return pl.ds(pl.multiple_of((unit[i] * Y + to) * R, R), R)

    def y_own(way, i, far):
        return acc[y_rows(i, lax.rem(y + (far if way == 0 else Y - far), Y)), :]

    def y_hop(way, i, part):
        src, dst = ysend.at[way, i, part], yrecv.at[way, i, part]
        if part == 1:
            src, dst = src.at[:, share[way]], dst.at[:, share[way]]
        return remote(src, dst, y_s.at[way, i, part], y_r.at[way, i, part], y_by[way, 1 + part % 2])

    def y_start(way, i, part):
        ysend[way, i, part] = y_own(way, i, (3, 4, 1)[part]).astype(BF16)
        y_hop(way, i, part).start()

    def y_relay(way, i):
        y_hop(way, i, 0).wait_recv()
        y_hop(way, i, 1).wait_recv()
        far = yrecv[way, i, 1, :, share[way]].astype(F32)
        none = jnp.zeros((R, F - far.shape[1]), F32)
        far = jnp.concatenate([far, none] if way == 0 else [none, far], axis=1)
        value = y_own(way, i, 2) + yrecv[way, i, 0].astype(F32) + far
        ysend[way, i, 3] = value.astype(BF16)
        y_hop(way, i, 3).start()

    def y_total(i):
        value = acc[y_rows(i, y), :]
        for part in (2, 3):
            for way in (0, 1):
                y_hop(way, i, part).wait_recv()
                value = value + yrecv[way, i, part].astype(F32)
        return value

    def drain_y():
        for way in (0, 1):
            for i in (0, 1):
                for part in range(4):
                    y_hop(way, i, part).wait_send()

    dw_batch(batch(NB - 1), NB == 1)


    for part in range(3):
        for way in (0, 1):
            y_start(way, 0, part)
    for way in (0, 1):
        y_relay(way, 0)
    for part in range(3):
        for way in (0, 1):
            y_start(way, 1, part)
    dx_step(4)

    hsend[...] = y_total(0).astype(BF16)

    @pl.when(h == 0)
    def _():
        pl.semaphore_wait(h_ready, 1)

    across = remote(hsend, hrecv, h_s, h_r, h_by)
    across.start()
    for way in (0, 1):
        y_relay(way, 1)
    dx_step(2)
    tu[...] = y_total(1)

    dx_sum[...] = pair(z)
    for way in (0, 1):
        dx_add(way, z)
    dx_out[...] = dx_sum[...].astype(BF16)

    drain_gather()
    drain_g()
    drain_dx()
    drain_y()

    across.wait_recv()
    factor = 1.0 / math.sqrt(H * Y * X * T)
    dw_out[...] = (tu[...] + hrecv[...].astype(F32)) * factor
    across.wait_send()


def body(n, mantissas, exponents, weight, cotangent):
    H, Y, X, Z, C, B, R, F = n.H, n.Y, n.X, n.Z, n.C, n.B, n.R, n.F
    HY = H * Y
    D = HY * X * R
    Q, T, S = D // X, Z * B * C, n.S
    NB, BC = Z // GROUP, GROUP * B
    BT = C * BC
    anywhere = pl.BlockSpec(memory_space=pl.ANY)
    hbm = pl.BlockSpec(memory_space=pltpu.HBM)
    vmem = pl.BlockSpec(memory_space=pltpu.VMEM)
    dma = pltpu.SemaphoreType.DMA
    out, dx, dw = pl.pallas_call(
        functools.partial(kernel, n),
        out_shape=(
            jax.ShapeDtypeStruct((NB, GROUP, C, B, F), BF16),
            jax.ShapeDtypeStruct((B, D), BF16),
            jax.ShapeDtypeStruct((R, F), F32),
        ),
        in_specs=[hbm] * 4,
        out_specs=(anywhere, vmem, vmem),
        scratch_shapes=[
            pltpu.VMEM((B, D), BF16),
            pltpu.VMEM((B, D // 128), jnp.int32),
            pltpu.VMEM((X, HY, R, F), BF16),
            pltpu.VMEM((HY, X, R, F), BF16),
            pltpu.VMEM((NB, C, GROUP, B, F), BF16),
            pltpu.VMEM((T, D), BF16),
            pltpu.VMEM((NB, 4, BT, Q), BF16),
            pltpu.VMEM((NB, 4, BT, F), BF16),
            pltpu.VMEM((NB, C, GROUP, B, F), BF16),
            pltpu.VMEM((T, D), BF16),
            pltpu.VMEM((Z * B, D), BF16),
            pltpu.VMEM((2, 2, Z, B, D), BF16),
            pltpu.VMEM((2, Z, B, D), BF16),
            pltpu.VMEM((B, D), F32),
            pltpu.VMEM((Q, F), F32),
            pltpu.VMEM((2, 2, 4, R, F), BF16),
            pltpu.VMEM((2, 2, 4, R, F), BF16),
            pltpu.VMEM((R, F), F32),
            pltpu.VMEM((R, F), BF16),
            pltpu.VMEM((R, F), BF16),
            dma((3 + X + 2 * C,)),
            dma((2, Z, S)),
            dma((2, Z, S)),
            dma((Z,)),
            dma((Z,)),
            dma((4,)),
            dma((4, NB)),
            dma((NB, 4)),
            dma((NB, 4)),
            dma((NB, 4)),
            dma((NB, 4)),
            dma((NB, X)),
            dma((NB, X)),
            dma((2, Z)),
            dma((2, 2, Z)),
            dma((2, 2, 4)),
            dma((2, 2, 4)),
            dma,
            dma,
            pltpu.SemaphoreType.REGULAR,
        ],
        compiler_params=pltpu.CompilerParams(
            collective_id=0, has_side_effects=True, vmem_limit_bytes=50 * 1024 * 1024
        ),
        cost_estimate=pl.CostEstimate(
            flops=6 * T * D * F, bytes_accessed=4 * D * F, transcendentals=T * F
        ),
    )(
        *(
            pltpu.with_memory_space_constraint(a, pltpu.HBM)
            for a in (
                mantissas,
                exponents,
                weight.reshape(HY, X, R, F),
                cotangent.reshape(NB, GROUP, C, B, F),
            )
        ),
    )
    return out.reshape(T, F), dx, dw


def solution(mesh, sizes=SIZES):
    n = SimpleNamespace(**vars(sizes), S=2)
    return jax.shard_map(
        functools.partial(body, n),
        mesh=mesh,
        in_specs=(
            P(("dp", "tensor"), None),
            P(("dp", "tensor"), None),
            P(None, "tensor"),
            P("dp", "tensor"),
        ),
        out_specs=(P("dp", "tensor"), P(("dp", "tensor"), None), P("dp", "tensor")),
        check_vma=False,
    )
```
